32 devices in a mesh: box: 8 (over z, x), sub: 4 (over y, core).
Axes of the slice: x: 2, y: 2, z: 4, core: 2. Of those that a mesh axis runs over, the one named last changes fastest.
Arguments:
- leaves: bfloat16 [1024, 16, 256], P(('box', 'sub')), may hold values from -6 to 6
- local_src: int32 [1024, 8], P(('box', 'sub')), may hold values from 0 to 31
- local_cls: int32 [1024, 8], P(('box', 'sub')), may hold values from 0 to 11
- send_box: int32 [32, 8, 2], P(('box', 'sub')), may hold values from 0 to 31
- recv_tgt: int32 [32, 8, 2], P(('box', 'sub')), may hold values from 0 to 31
- recv_cls: int32 [32, 8, 2], P(('box', 'sub')), may hold values from 0 to 11
- recv_live: int32 [32, 8, 2], P(('box', 'sub')), may hold values from 0 to 1, as said below
- translation: bfloat16 [12, 256, 256], replicated, may hold values from -0.125 to 0.125
- up_maps: bfloat16 [4, 8, 256, 256], P('sub'), may hold values from -0.09375 to 0.09375
- down_maps: bfloat16 [4, 8, 256, 256], P('sub'), may hold values from -0.375 to 0.375
- coupling: float32 [8, 8], replicated, may hold values from -2 to 2
Outputs:
- pressure_adjoint: bfloat16 [1024, 16, 256], P(('box', 'sub'))
The draws below stay inside these ranges and needn't reach their ends.
Inputs may be any that keep to these rules, and one draw needn't show every extreme that they name: `recv_live`: among the devices with one index along sub, one drawn from the seed has every received slot live.
All inputs are finite; a program needn't handle non-finite values.
Results may differ from the reference program's by a relative error of at most 0.01.
Values may be sent and summed in bfloat16 or wider, within the bound.
A program may use at most 64 MiB of HBM per device.

```python
import jax
import jax.numpy as jnp
from jax import lax

P_SIZE = 256
S = 16
BOX_DEV = 32
NLOC = 8
CAP = 2
CL = 12
BOXES = 1024
N_BOX = 8
N_SUB = 4


def draw_recv_live(key, part):
    key = jax.random.fold_in(key, 5)
    key_pct, key_busy, key_roll = jax.random.split(key, 3)
    device_count = N_BOX * N_SUB
    percent = jax.random.randint(key_pct, (device_count, 1, 1), 5, 80)
    busiest = jax.random.randint(key_busy, (N_SUB,), 0, N_BOX)
    devices = jnp.arange(device_count, dtype=jnp.int32)
    filled = devices // N_SUB == busiest[devices % N_SUB]
    rolled = jax.random.randint(key_roll, (device_count, N_BOX, CAP), 0, 100)
    live_flags = jnp.where(filled[:, None, None], True, rolled < percent)
    return live_flags.astype(jnp.int32)


def place_ends(drawn, stream_key, low, largest):
    place = [jax.random.randint(jax.random.fold_in(stream_key, axis), (), 0, length) for axis, length in enumerate(drawn.shape)]
    longest = drawn.shape.index(max(drawn.shape))
    next_to = place[:longest] + [(place[longest] + 1) % drawn.shape[longest]] + place[longest + 1:]
    return drawn.at[tuple(place)].set(low).at[tuple(next_to)].set(largest)


def block_scale(stream_key, shape, shards, least, largest):
    level = 1.0
    for dim, blocks in shards:
        draws = jax.random.uniform(jax.random.fold_in(jax.random.fold_in(stream_key, 6), dim), (blocks,), jnp.float32, least / len(shards), largest / len(shards))
        level = level * jnp.repeat(jnp.exp(draws), shape[dim] // blocks).reshape((-1,) + (1,) * (len(shape) - 1 - dim))
    return level


def bell_draw(stream_key, extent, scale, bound, shards=(), held_as=jnp.bfloat16):
    drawn = scale * jax.random.normal(stream_key, extent, jnp.float32)
    if shards:
        drawn = drawn * block_scale(stream_key, extent, shards, -0.22, 0.18)
    return jnp.clip(drawn, -bound, bound).astype(held_as)


def setup_inputs(seed: int = 0) -> dict:
    keys = jax.random.split(jax.random.key(seed), 12)
    return {
        "leaves": bell_draw(keys[0], (BOXES, S, P_SIZE), 1.0, 6.0, ((0, 32),)),
        "local_src": place_ends(jax.random.randint(keys[1], (BOXES, NLOC), 0, BOX_DEV), jax.random.fold_in(keys[1], 1), 0, BOX_DEV - 1).astype(jnp.int32),
        "local_cls": place_ends(jax.random.randint(keys[2], (BOXES, NLOC), 0, CL), jax.random.fold_in(keys[2], 1), 0, CL - 1).astype(jnp.int32),
        "send_box": place_ends(jax.random.randint(keys[3], (N_BOX * N_SUB, N_BOX, CAP), 0, BOX_DEV), jax.random.fold_in(keys[3], 1), 0, BOX_DEV - 1).astype(jnp.int32),
        "recv_tgt": place_ends(jax.random.randint(keys[4], (N_BOX * N_SUB, N_BOX, CAP), 0, BOX_DEV), jax.random.fold_in(keys[4], 1), 0, BOX_DEV - 1).astype(jnp.int32),
        "recv_cls": place_ends(jax.random.randint(keys[5], (N_BOX * N_SUB, N_BOX, CAP), 0, CL), jax.random.fold_in(keys[5], 1), 0, CL - 1).astype(jnp.int32),
        "recv_live": draw_recv_live(jax.random.fold_in(keys[11], 71), 0),
        "translation": bell_draw(keys[7], (CL, P_SIZE, P_SIZE), (10 * P_SIZE) ** -0.5, 0.125),
        "up_maps": bell_draw(keys[8], (N_SUB, 8, P_SIZE, P_SIZE), (P_SIZE * BOX_DEV * N_SUB // 8) ** -0.5, 0.09375, ((0, 4),)),
        "down_maps": bell_draw(keys[9], (N_SUB, 8, P_SIZE, P_SIZE), P_SIZE ** -0.5, 0.375, ((0, 4),)),
        "coupling": bell_draw(keys[10], (N_BOX, N_BOX), N_BOX ** -0.5, 2.0, (), jnp.float32),
    }


def reference(leaves, local_src, local_cls, send_box, recv_tgt, recv_cls, recv_live, translation, up_maps, down_maps, coupling):
    device_count = N_BOX * N_SUB
    child_sum = jnp.sum(leaves.astype(jnp.float32).reshape(device_count, BOX_DEV // 8, 8, S, P_SIZE), axis=1).astype(jnp.bfloat16)
    child_sum = child_sum.reshape(N_BOX, N_SUB, 8, S, P_SIZE)
    partial_value = jnp.einsum('ijcsp,jcqp->ijsq', child_sum.astype(jnp.float32), up_maps.astype(jnp.float32))
    top_sum = jnp.sum(partial_value, axis=1)
    far_sum = jnp.einsum('ik,ksp->isp', coupling, top_sum, precision=lax.Precision.HIGHEST).astype(jnp.bfloat16)
    far_field = jnp.einsum('isp,jcqp->ijcsq', far_sum.astype(jnp.float32), down_maps.astype(jnp.float32))
    far_field = far_field.reshape(device_count, 8, S, P_SIZE)
    own_all = leaves.reshape(device_count, BOX_DEV, S, P_SIZE)
    sender_box = send_box.reshape(N_BOX, N_SUB, N_BOX, CAP)
    local_src_dev = local_src.reshape(device_count, BOX_DEV, NLOC)
    local_cls_dev = local_cls.reshape(device_count, BOX_DEV, NLOC)
    transl_wide = translation.astype(jnp.float32)

    def per_device(packed):
        device, far_here = packed
        box_index = device // N_SUB
        sub_index = device % N_SUB
        by_sub = lax.dynamic_index_in_dim(sender_box, sub_index, 1, False)
        picked = lax.dynamic_index_in_dim(by_sub, box_index, 1, False)
        anchor = (jnp.arange(N_BOX, dtype=jnp.int32) * N_SUB + sub_index)[:, None] * BOX_DEV + picked
        arrived = leaves[anchor]
        own_boxes = lax.dynamic_index_in_dim(own_all, device, 0, False)
        near_src = lax.dynamic_index_in_dim(local_src_dev, device, 0, False)
        near_cls = lax.dynamic_index_in_dim(local_cls_dev, device, 0, False)
        near_rows = own_boxes[near_src]
        targets = lax.dynamic_index_in_dim(recv_tgt, device, 0, False)
        classes = lax.dynamic_index_in_dim(recv_cls, device, 0, False)
        live_flags = lax.dynamic_index_in_dim(recv_live, device, 0, False)
        stacked = jnp.concatenate([arrived.reshape(-1, S * P_SIZE), near_rows.reshape(-1, S * P_SIZE)], axis=0).astype(jnp.float32)
        weights = jnp.concatenate([live_flags.reshape(-1), jnp.ones((BOX_DEV * NLOC,), jnp.int32)]).astype(jnp.float32)
        own_ids = jnp.arange(BOX_DEV, dtype=jnp.int32)[:, None]
        segment_ids = jnp.concatenate([(classes * BOX_DEV + targets).reshape(-1), (near_cls * BOX_DEV + own_ids).reshape(-1)])
        summed = jax.ops.segment_sum(stacked * weights[:, None], segment_ids, num_segments=CL * BOX_DEV)
        grouped = summed.astype(jnp.bfloat16).reshape(CL, BOX_DEV, S, P_SIZE)
        near_field = jnp.einsum('cbsp,cqp->bsq', grouped.astype(jnp.float32), transl_wide)
        total = near_field.reshape(BOX_DEV // 8, 8, S, P_SIZE) + far_here[None]
        return total.reshape(BOX_DEV, S, P_SIZE).astype(jnp.bfloat16)

    result = lax.map(per_device, (jnp.arange(device_count, dtype=jnp.int32), far_field))
    return result.reshape(BOXES, S, P_SIZE)
```

```python
import functools

import jax
import jax.numpy as jnp
from jax import lax
from jax.experimental import pallas as pl
from jax.experimental.pallas import tpu as pltpu
from jax.sharding import PartitionSpec as P

MESH = pl.DeviceIdType.MESH
F32 = jnp.float32
BF16 = jnp.bfloat16


def dot_nt(a, b):
    return lax.dot_general(a, b, (((1,), (1,)), ((), ())), preferred_element_type=F32)


def swap_matrix(outer, inner):
    size = outer * inner
    row = lax.broadcasted_iota(jnp.int32, (size, 1), 0)
    source = (row % inner) * outer + row // inner
    column = lax.broadcasted_iota(jnp.int32, (size, size), 1)
    return jnp.where(column == source, 1.0, 0.0).astype(BF16)


def kernel(
    nb,
    ns,
    leaves_hbm,
    src_ref,
    cls_ref,
    send_box,
    recv_tgt,
    recv_cls,
    recv_live,
    trans_hbm,
    up_hbm,
    down_hbm,
    coupling,
    out_ref,
    leaves,
    trans,
    up,
    down,
    outgoing,
    arrived,
    part_out,
    parts,
    top_out,
    tops,
    mixed,
    counts,
    grouped,
    near,
    load_sem,
    slot_send,
    slot_recv,
    part_send,
    part_recv,
    top_send,
    top_recv,
):
    box = lax.axis_index("box")
    sub = lax.axis_index("sub")
    boxes, rhs, width = leaves.shape
    cap = outgoing.shape[1]
    classes = trans.shape[0]
    children = up.shape[0]
    slots = nb * cap
    depth = boxes + slots

    def box_peer(d):
        return (lax.rem(box + d, nb), sub)

    def sub_peer(d):
        return (box, lax.rem(sub + d, ns))

    def over(count, body):
        if count <= 16:
            for d in range(1, count):
                body(d)
        else:
            pl.loop(1, count)(body)

    barrier = pltpu.get_barrier_semaphore()
    over(ns, lambda d: pl.semaphore_signal(barrier, inc=1, device_id=sub_peer(d), device_id_type=MESH))
    over(nb, lambda d: pl.semaphore_signal(barrier, inc=1, device_id=box_peer(d), device_id_type=MESH))

    loads = [
        pltpu.make_async_copy(leaves_hbm, leaves, load_sem.at[0]),
        pltpu.make_async_copy(up_hbm.at[0], up, load_sem.at[1]),
        pltpu.make_async_copy(trans_hbm, trans, load_sem.at[2]),
        pltpu.make_async_copy(down_hbm.at[0], down, load_sem.at[3]),
    ]
    for load in loads:
        load.start()

    lane = lax.broadcasted_iota(jnp.int32, (1, depth), 1)
    slot_code = jnp.full((1, depth), -1, jnp.int32)

    def add_slot(d, c, code):
        k = lax.rem(box - d + nb, nb)
        value = recv_cls[0, k, c] * boxes + recv_tgt[0, k, c]
        value = jnp.where(recv_live[0, k, c] != 0, value, -1)
        return jnp.where(lane == boxes + d * cap + c, value, code)

    if nb <= 16:
        for d in range(nb):
            for c in range(cap):
                slot_code = add_slot(d, c, slot_code)
    else:
        def add_peer(d, code):
            for c in range(cap):
                code = add_slot(d, c, code)
            return code

        slot_code = lax.fori_loop(0, nb, add_peer, slot_code)
    own_code = cls_ref[...] * depth + src_ref[...]
    target = lax.broadcasted_iota(jnp.int32, (boxes, depth), 0)
    for q in range(classes):
        total = jnp.where(slot_code == q * boxes + target, 1.0, 0.0)
        for n in range(own_code.shape[1]):
            total += jnp.where(own_code[:, n : n + 1] == q * depth + lane, 1.0, 0.0)
        counts[q * boxes : (q + 1) * boxes, :] = total.astype(BF16)

    loads[0].wait()

    if nb <= 16:
        for d in range(nb):
            for c in range(cap):
                k = lax.rem(box + d, nb)
                outgoing[d, c] = leaves[send_box[0, k, c]]
    else:
        @pl.loop(0, nb)
        def _(d):
            for c in range(cap):
                outgoing[d, c] = leaves[send_box[0, lax.rem(box + d, nb), c]]

    for c in range(cap):
        arrived[0, c] = outgoing[0, c]

    child = leaves[0:children].astype(F32)
    for g in range(1, boxes // children):
        child += leaves[g * children : (g + 1) * children].astype(F32)
    child = child.astype(BF16)

    loads[1].wait()
    part = dot_nt(child[0], up[0])
    for m in range(1, children):
        part += dot_nt(child[m], up[m])
    part_out[...] = part.astype(BF16)

    pl.semaphore_wait(barrier, nb + ns - 2)

    def part_copy(d):
        return pltpu.make_async_remote_copy(
            src_ref=part_out,
            dst_ref=parts.at[d],
            send_sem=part_send.at[d],
            recv_sem=part_recv.at[d],
            device_id=sub_peer(d),
            device_id_type=MESH,
        )

    def slot_copy(d):
        return pltpu.make_async_remote_copy(
            src_ref=outgoing.at[d],
            dst_ref=arrived.at[d],
            send_sem=slot_send.at[d],
            recv_sem=slot_recv.at[d],
            device_id=box_peer(d),
            device_id_type=MESH,
        )

    def top_copy(d):
        return pltpu.make_async_remote_copy(
            src_ref=top_out,
            dst_ref=tops.at[d],
            send_sem=top_send.at[d],
            recv_sem=top_recv.at[d],
            device_id=box_peer(d),
            device_id_type=MESH,
        )

    over(ns, lambda d: part_copy(d).start())
    over(nb, lambda d: slot_copy(d).start())

    mixed[:, 0:boxes, :] = (
        jnp.dot(
            swap_matrix(rhs, boxes),
            leaves[...].reshape(boxes * rhs, width),
            preferred_element_type=F32,
        )
        .astype(BF16)
        .reshape(rhs, boxes, width)
    )

    top = part
    over(ns, lambda d: part_copy(d).wait_recv())
    for d in range(1, ns):
        top += parts[d].astype(F32)
    top_out[...] = top.astype(BF16)
    over(nb, lambda d: top_copy(d).start())

    over(nb, lambda d: slot_copy(d).wait_recv())
    group = 16
    swap_slots = swap_matrix(rhs, group)
    per_group = group // cap
    for g in range(slots // group):
        rows = arrived[g * per_group : (g + 1) * per_group].reshape(group * rhs, width)
        mixed[:, boxes + g * group : boxes + (g + 1) * group, :] = (
            jnp.dot(swap_slots, rows, preferred_element_type=F32)
            .astype(BF16)
            .reshape(rhs, group, width)
        )

    for s in range(rhs):
        held = jnp.dot(counts[...], mixed[s], preferred_element_type=F32).astype(BF16)
        grouped[:, s * boxes : (s + 1) * boxes, :] = held.reshape(classes, boxes, width)

    loads[2].wait()
    total = dot_nt(grouped[0], trans[0])
    for q in range(1, classes):
        total += dot_nt(grouped[q], trans[q])
    high = total.astype(BF16)
    low = (total - high.astype(F32)).astype(BF16)
    back = swap_matrix(boxes, rhs)
    near[...] = (
        jnp.dot(back, high, preferred_element_type=F32)
        + jnp.dot(back, low, preferred_element_type=F32)
    ).reshape(boxes, rhs, width)

    loads[3].wait()
    over(nb, lambda d: top_copy(d).wait_recv())
    far = coupling[box, box] * top
    if nb <= 16:
        for d in range(1, nb):
            far += coupling[box, lax.rem(box - d + nb, nb)] * tops[d].astype(F32)
    else:
        far = lax.fori_loop(
            1,
            nb,
            lambda d, far: far + coupling[box, lax.rem(box - d + nb, nb)] * tops[d].astype(F32),
            far,
        )
    far = far.astype(BF16)
    for m in range(children):
        field = dot_nt(far, down[m])
        for g in range(boxes // children):
            b = g * children + m
            out_ref[b] = (near[b] + field).astype(BF16)

    over(ns, lambda d: part_copy(d).wait_send())
    over(nb, lambda d: slot_copy(d).wait_send())
    over(nb, lambda d: top_copy(d).wait_send())


def local(nb, ns, *args):
    leaves, local_src, local_cls, send_box, recv_tgt, recv_cls, recv_live = args[:7]
    translation, up_maps, down_maps, coupling = args[7:]
    boxes, rhs, width = leaves.shape
    cap = send_box.shape[2]
    classes = translation.shape[0]
    depth = boxes + nb * cap
    vmem = pl.BlockSpec(memory_space=pltpu.VMEM)
    smem = pl.BlockSpec(memory_space=pltpu.SMEM)
    hbm = pl.BlockSpec(memory_space=pl.ANY)
    dma = pltpu.SemaphoreType.DMA
    return pl.pallas_call(
        functools.partial(kernel, nb, ns),
        out_shape=jax.ShapeDtypeStruct(leaves.shape, BF16),
        in_specs=[hbm, vmem, vmem, smem, smem, smem, smem, hbm, hbm, hbm, smem],
        out_specs=vmem,
        scratch_shapes=[
            pltpu.VMEM((boxes, rhs, width), BF16),
            pltpu.VMEM(translation.shape, BF16),
            pltpu.VMEM(up_maps.shape[1:], BF16),
            pltpu.VMEM(down_maps.shape[1:], BF16),
            pltpu.VMEM((nb, cap, rhs, width), BF16),
            pltpu.VMEM((nb, cap, rhs, width), BF16),
            pltpu.VMEM((rhs, width), BF16),
            pltpu.VMEM((ns, rhs, width), BF16),
            pltpu.VMEM((rhs, width), BF16),
            pltpu.VMEM((nb, rhs, width), BF16),
            pltpu.VMEM((rhs, depth, width), BF16),
            pltpu.VMEM((classes * boxes, depth), BF16),
            pltpu.VMEM((classes, rhs * boxes, width), BF16),
            pltpu.VMEM((boxes, rhs, width), F32),
            dma((4,)),
            dma((nb,)),
            dma((nb,)),
            dma((ns,)),
            dma((ns,)),
            dma((nb,)),
            dma((nb,)),
        ],
        compiler_params=pltpu.CompilerParams(
            collective_id=0, has_side_effects=True, vmem_limit_bytes=48 * 1024 * 1024
        ),
    )(*args)


def solution(mesh):
    dev = ("box", "sub")
    in_specs = (
        P(dev, None, None),
        P(dev, None),
        P(dev, None),
        P(dev, None, None),
        P(dev, None, None),
        P(dev, None, None),
        P(dev, None, None),
        P(),
        P("sub", None, None, None),
        P("sub", None, None, None),
        P(),
    )
    return jax.shard_map(
        functools.partial(local, mesh.shape["box"], mesh.shape["sub"]),
        mesh=mesh,
        in_specs=in_specs,
        out_specs=P(dev, None, None),
        check_vma=False,
    )
```

```python
import functools

import jax
import jax.numpy as jnp
from jax import lax
from jax.experimental import pallas as pl
from jax.experimental.pallas import tpu as pltpu
from jax.sharding import PartitionSpec as P

MESH = pl.DeviceIdType.MESH
F32 = jnp.float32
BF16 = jnp.bfloat16


def dot_nt(a, b):
    return lax.dot_general(a, b, (((1,), (1,)), ((), ())), preferred_element_type=F32)


def swap_matrix(outer, inner):
    size = outer * inner
    row = lax.broadcasted_iota(jnp.int32, (size, 1), 0)
    source = (row % inner) * outer + row // inner
    column = lax.broadcasted_iota(jnp.int32, (size, size), 1)
    return jnp.where(column == source, 1.0, 0.0).astype(BF16)


def kernel(
    nb,
    ns,
    leaves_hbm,
    src_hbm,
    cls_hbm,
    send_hbm,
    tgt_hbm,
    rcls_hbm,
    live_hbm,
    trans_hbm,
    up_hbm,
    down_hbm,
    coupling_hbm,
    out_ref,
    src_ref,
    cls_ref,
    send_box,
    recv_tgt,
    recv_cls,
    recv_live,
    coupling,
    leaves,
    trans,
    up,
    down,
    outgoing,
    arrived,
    part_out,
    parts,
    top_out,
    tops,
    mixed,
    counts,
    grouped,
    near,
    swap_in,
    swap_slots,
    swap_back,
    load_sem,
    slot_send,
    slot_recv,
    part_send,
    part_recv,
    top_send,
    top_recv,
):
    box = lax.axis_index("box")
    sub = lax.axis_index("sub")
    boxes, rhs, width = leaves.shape
    cap = outgoing.shape[1]
    classes = trans.shape[0]
    children = up.shape[0]
    slots = nb * cap
    depth = boxes + slots

    def box_peer(d):
        return (lax.rem(box + d, nb), sub)

    def sub_peer(d):
        return (box, lax.rem(sub + d, ns))

    def over(count, body):
        if count <= 16:
            for d in range(1, count):
                body(d)
        else:
            pl.loop(1, count)(body)

    barrier = pltpu.get_barrier_semaphore()
    over(ns, lambda d: pl.semaphore_signal(barrier, inc=1, device_id=sub_peer(d), device_id_type=MESH))
    over(nb, lambda d: pl.semaphore_signal(barrier, inc=1, device_id=box_peer(d), device_id_type=MESH))

    pairs = (
        (leaves_hbm, leaves),
        (send_hbm, send_box),
        (up_hbm.at[0], up),
        (src_hbm, src_ref),
        (cls_hbm, cls_ref),
        (tgt_hbm, recv_tgt),
        (rcls_hbm, recv_cls),
        (live_hbm, recv_live),
        (coupling_hbm, coupling),
        (trans_hbm, trans),
        (down_hbm.at[0], down),
    )
    loads = [pltpu.make_async_copy(a, b, load_sem.at[n]) for n, (a, b) in enumerate(pairs)]
    for load in loads:
        load.start()

    group = 16
    swap_in[...] = swap_matrix(rhs, boxes)
    swap_slots[...] = swap_matrix(rhs, group)
    swap_back[...] = swap_matrix(boxes, rhs)

    loads[0].wait()
    child = leaves[0:children].astype(F32)
    for g in range(1, boxes // children):
        child += leaves[g * children : (g + 1) * children].astype(F32)
    child = child.astype(BF16)

    loads[1].wait()
    if nb <= 16:
        for d in range(nb):
            for c in range(cap):
                outgoing[d, c] = leaves[send_box[0, c, lax.rem(box + d, nb)]]
    else:

        @pl.loop(0, nb)
        def _(d):
            for c in range(cap):
                outgoing[d, c] = leaves[send_box[0, c, lax.rem(box + d, nb)]]

    for c in range(cap):
        arrived[0, c] = outgoing[0, c]

    loads[2].wait()
    part = dot_nt(child[0], up[0])
    for m in range(1, children):
        part += dot_nt(child[m], up[m])
    part_out[...] = part.astype(BF16)

    pl.semaphore_wait(barrier, nb + ns - 2)

    def part_copy(d):
        return pltpu.make_async_remote_copy(
            src_ref=part_out,
            dst_ref=parts.at[d],
            send_sem=part_send.at[d],
            recv_sem=part_recv.at[d],
            device_id=sub_peer(d),
            device_id_type=MESH,
        )

    def slot_copy(d):
        return pltpu.make_async_remote_copy(
            src_ref=outgoing.at[d],
            dst_ref=arrived.at[d],
            send_sem=slot_send.at[d],
            recv_sem=slot_recv.at[d],
            device_id=box_peer(d),
            device_id_type=MESH,
        )

    def top_copy(d):
        return pltpu.make_async_remote_copy(
            src_ref=top_out,
            dst_ref=tops.at[d],
            send_sem=top_send.at[d],
            recv_sem=top_recv.at[d],
            device_id=box_peer(d),
            device_id_type=MESH,
        )

    over(ns, lambda d: part_copy(d).start())
    over(nb, lambda d: slot_copy(d).start())

    mixed[:, 0:boxes, :] = (
        jnp.dot(
            swap_in[...],
            leaves[...].reshape(boxes * rhs, width),
            preferred_element_type=F32,
        )
        .astype(BF16)
        .reshape(rhs, boxes, width)
    )

    top = part
    over(ns, lambda d: part_copy(d).wait_recv())
    for d in range(1, ns):
        top += parts[d].astype(F32)
    top_out[...] = top.astype(BF16)
    over(nb, lambda d: top_copy(d).start())


    for load in loads[3:9]:
        load.wait()
    lane = lax.broadcasted_iota(jnp.int32, (1, depth), 1)

    def add_slot(d, c, code):
        k = lax.rem(box - d + nb, nb)
        value = recv_cls[0, c, k] * boxes + recv_tgt[0, c, k]
        value = jnp.where(recv_live[0, c, k] != 0, value, -1)
        return jnp.where(lane == boxes + d * cap + c, value, code)

    def add_peer(d, code):
        for c in range(cap):
            code = add_slot(d, c, code)
        return code

    slot_code = jnp.full((1, depth), -1, jnp.int32)
    if nb <= 16:
        for d in range(nb):
            slot_code = add_peer(d, slot_code)
    else:
        slot_code = lax.fori_loop(0, nb, add_peer, slot_code)
    own_code = jnp.transpose(cls_ref[...] * depth + src_ref[...])
    target = lax.broadcasted_iota(jnp.int32, (boxes, depth), 0)
    for q in range(classes):
        total = jnp.where(slot_code == q * boxes + target, 1.0, 0.0)
        for n in range(own_code.shape[1]):
            total += jnp.where(own_code[:, n : n + 1] == q * depth + lane, 1.0, 0.0)
        counts[q * boxes : (q + 1) * boxes, :] = total.astype(BF16)

    over(nb, lambda d: slot_copy(d).wait_recv())
    per_group = group // cap
    for g in range(slots // group):
        rows = arrived[g * per_group : (g + 1) * per_group].reshape(group * rhs, width)
        mixed[:, boxes + g * group : boxes + (g + 1) * group, :] = (
            jnp.dot(swap_slots[...], rows, preferred_element_type=F32)
            .astype(BF16)
            .reshape(rhs, group, width)
        )

    for s in range(rhs):
        held = jnp.dot(counts[...], mixed[s], preferred_element_type=F32).astype(BF16)
        grouped[:, s * boxes : (s + 1) * boxes, :] = held.reshape(classes, boxes, width)

    loads[9].wait()
    total = dot_nt(grouped[0], trans[0])
    for q in range(1, classes):
        total += dot_nt(grouped[q], trans[q])
    high = total.astype(BF16)
    low = (total - high.astype(F32)).astype(BF16)
    near[...] = (
        jnp.dot(swap_back[...], high, preferred_element_type=F32)
        + jnp.dot(swap_back[...], low, preferred_element_type=F32)
    ).reshape(boxes, rhs, width)

    loads[10].wait()
    over(nb, lambda d: top_copy(d).wait_recv())
    far = coupling[box, box] * top
    if nb <= 16:
        for d in range(1, nb):
            far += coupling[box, lax.rem(box - d + nb, nb)] * tops[d].astype(F32)
    else:
        far = lax.fori_loop(
            1,
            nb,
            lambda d, far: far + coupling[box, lax.rem(box - d + nb, nb)] * tops[d].astype(F32),
            far,
        )
    far = far.astype(BF16)
    for m in range(children):
        field = dot_nt(far, down[m])
        for g in range(boxes // children):
            b = g * children + m
            out_ref[b] = (near[b] + field).astype(BF16)

    over(ns, lambda d: part_copy(d).wait_send())
    over(nb, lambda d: slot_copy(d).wait_send())
    over(nb, lambda d: top_copy(d).wait_send())


def local(nb, ns, *args):
    leaves, local_src, local_cls, send_box, recv_tgt, recv_cls, recv_live = args[:7]
    translation, up_maps, down_maps, coupling = args[7:]
    boxes, rhs, width = leaves.shape
    cap = send_box.shape[2]
    classes = translation.shape[0]
    depth = boxes + nb * cap
    rows = boxes * rhs
    vmem = pl.BlockSpec(memory_space=pltpu.VMEM)
    hbm = pl.BlockSpec(memory_space=pltpu.HBM)
    dma = pltpu.SemaphoreType.DMA
    int_vmem = pltpu.VMEM(local_src.shape[::-1], jnp.int32)
    int_smem = pltpu.SMEM((1, cap, nb), jnp.int32)
    return pl.pallas_call(
        functools.partial(kernel, nb, ns),
        out_shape=jax.ShapeDtypeStruct(leaves.shape, BF16),
        in_specs=[hbm] * 11,
        out_specs=vmem,
        scratch_shapes=[
            int_vmem,
            int_vmem,
            int_smem,
            int_smem,
            int_smem,
            int_smem,
            pltpu.SMEM(coupling.shape, F32),
            pltpu.VMEM((boxes, rhs, width), BF16),
            pltpu.VMEM(translation.shape, BF16),
            pltpu.VMEM(up_maps.shape[1:], BF16),
            pltpu.VMEM(down_maps.shape[1:], BF16),
            pltpu.VMEM((nb, cap, rhs, width), BF16),
            pltpu.VMEM((nb, cap, rhs, width), BF16),
            pltpu.VMEM((rhs, width), BF16),
            pltpu.VMEM((ns, rhs, width), BF16),
            pltpu.VMEM((rhs, width), BF16),
            pltpu.VMEM((nb, rhs, width), BF16),
            pltpu.VMEM((rhs, depth, width), BF16),
            pltpu.VMEM((classes * boxes, depth), BF16),
            pltpu.VMEM((classes, rhs * boxes, width), BF16),
            pltpu.VMEM((boxes, rhs, width), F32),
            pltpu.VMEM((rows, rows), BF16),
            pltpu.VMEM((16 * rhs, 16 * rhs), BF16),
            pltpu.VMEM((rows, rows), BF16),
            dma((11,)),
            dma((nb,)),
            dma((nb,)),
            dma((ns,)),
            dma((ns,)),
            dma((nb,)),
            dma((nb,)),
        ],
        compiler_params=pltpu.CompilerParams(
            collective_id=0, has_side_effects=True, vmem_limit_bytes=64 * 1024 * 1024
        ),
    )(
        leaves,
        local_src.T,
        local_cls.T,
        *(jnp.transpose(a, (0, 2, 1)) for a in (send_box, recv_tgt, recv_cls, recv_live)),
        translation,
        up_maps,
        down_maps,
        coupling,
    )


def solution(mesh):
    dev = ("box", "sub")
    in_specs = (
        P(dev, None, None),
        P(dev, None),
        P(dev, None),
        P(dev, None, None),
        P(dev, None, None),
        P(dev, None, None),
        P(dev, None, None),
        P(),
        P("sub", None, None, None),
        P("sub", None, None, None),
        P(),
    )
    return jax.shard_map(
        functools.partial(local, mesh.shape["box"], mesh.shape["sub"]),
        mesh=mesh,
        in_specs=in_specs,
        out_specs=P(dev, None, None),
        check_vma=False,
    )
```

```python
import functools

import jax
import jax.numpy as jnp
from jax import lax
from jax.experimental import pallas as pl
from jax.experimental.pallas import tpu as pltpu
from jax.sharding import PartitionSpec as P

MESH = pl.DeviceIdType.MESH
F32 = jnp.float32
BF16 = jnp.bfloat16


def dot_nt(a, b):
    return lax.dot_general(a, b, (((1,), (1,)), ((), ())), preferred_element_type=F32)


def swap_matrix(outer, inner):
    size = outer * inner
    row = lax.broadcasted_iota(jnp.int32, (size, 1), 0)
    source = (row % inner) * outer + row // inner
    column = lax.broadcasted_iota(jnp.int32, (size, size), 1)
    return jnp.where(column == source, 1.0, 0.0).astype(BF16)


def kernel(
    nb,
    ns,
    leaves_hbm,
    src_hbm,
    cls_hbm,
    send_hbm,
    tgt_hbm,
    rcls_hbm,
    live_hbm,
    trans_hbm,
    up_hbm,
    down_hbm,
    coupling_hbm,
    out_ref,
    src_ref,
    cls_ref,
    send_box,
    recv_tgt,
    recv_cls,
    recv_live,
    coupling,
    leaves,
    trans,
    up,
    down,
    outgoing,
    arrived,
    part_out,
    parts,
    top_out,
    tops,
    mixed,
    counts,
    grouped,
    near,
    swap_in,
    swap_slots,
    swap_back,
    load_sem,
    slot_send,
    slot_recv,
    part_send,
    part_recv,
    top_send,
    top_recv,
):
    box = lax.axis_index("box")
    sub = lax.axis_index("sub")
    boxes, rhs, width = leaves.shape
    cap = outgoing.shape[1]
    classes = trans.shape[0]
    children = up.shape[0]
    slots = nb * cap
    depth = boxes + slots

    def box_peer(d):
        return (lax.rem(box + d, nb), sub)

    def sub_peer(d):
        return (box, lax.rem(sub + d, ns))

    def over(count, body):
        if count <= 16:
            for d in range(1, count):
                body(d)
        else:
            pl.loop(1, count)(body)

    barrier = pltpu.get_barrier_semaphore()
    over(ns, lambda d: pl.semaphore_signal(barrier, inc=1, device_id=sub_peer(d), device_id_type=MESH))
    over(nb, lambda d: pl.semaphore_signal(barrier, inc=1, device_id=box_peer(d), device_id_type=MESH))

    pairs = (
        (leaves_hbm, leaves),
        (send_hbm, send_box),
        (up_hbm.at[0], up),
        (src_hbm, src_ref),
        (cls_hbm, cls_ref),
        (tgt_hbm, recv_tgt),
        (rcls_hbm, recv_cls),
        (live_hbm, recv_live),
        (coupling_hbm, coupling),
        (trans_hbm, trans),
        (down_hbm.at[0], down),
    )
    loads = [pltpu.make_async_copy(a, b, load_sem.at[n]) for n, (a, b) in enumerate(pairs)]
    for load in loads:
        load.start()

    group = 16
    swap_in[...] = swap_matrix(rhs, boxes)
    swap_slots[...] = swap_matrix(rhs, group)
    swap_back[...] = swap_matrix(boxes, rhs)

    loads[0].wait()
    child = leaves[0:children].astype(F32)
    for g in range(1, boxes // children):
        child += leaves[g * children : (g + 1) * children].astype(F32)
    child = child.astype(BF16)

    loads[1].wait()
    if nb <= 16:
        for d in range(nb):
            for c in range(cap):
                outgoing[d, c] = leaves[send_box[0, c, lax.rem(box + d, nb)]]
    else:

        @pl.loop(0, nb)
        def _(d):
            for c in range(cap):
                outgoing[d, c] = leaves[send_box[0, c, lax.rem(box + d, nb)]]

    for c in range(cap):
        arrived[0, c] = outgoing[0, c]

    loads[2].wait()
    part = dot_nt(child[0], up[0])
    for m in range(1, children):
        part += dot_nt(child[m], up[m])
    part_out[...] = part.astype(BF16)

    pl.semaphore_wait(barrier, nb + ns - 2)

    def part_copy(d):
        return pltpu.make_async_remote_copy(
            src_ref=part_out,
            dst_ref=parts.at[d],
            send_sem=part_send.at[d],
            recv_sem=part_recv.at[d],
            device_id=sub_peer(d),
            device_id_type=MESH,
        )

    def slot_copy(d):
        return pltpu.make_async_remote_copy(
            src_ref=outgoing.at[d],
            dst_ref=arrived.at[d],
            send_sem=slot_send.at[d],
            recv_sem=slot_recv.at[d],
            device_id=box_peer(d),
            device_id_type=MESH,
        )

    def top_copy(d):
        return pltpu.make_async_remote_copy(
            src_ref=top_out,
            dst_ref=tops.at[d],
            send_sem=top_send.at[d],
            recv_sem=top_recv.at[d],
            device_id=box_peer(d),
            device_id_type=MESH,
        )

    over(ns, lambda d: part_copy(d).start())
    over(nb, lambda d: slot_copy(d).start())

    mixed[:, 0:boxes, :] = (
        jnp.dot(
            swap_in[...],
            leaves[...].reshape(boxes * rhs, width),
            preferred_element_type=F32,
        )
        .astype(BF16)
        .reshape(rhs, boxes, width)
    )

    top = part
    over(ns, lambda d: part_copy(d).wait_recv())
    for d in range(1, ns):
        top += parts[d].astype(F32)
    top_out[...] = top.astype(BF16)
    over(nb, lambda d: top_copy(d).start())


    for load in loads[3:9]:
        load.wait()
    lane = lax.broadcasted_iota(jnp.int32, (1, depth), 1)

    def add_slot(d, c, code):
        k = lax.rem(box - d + nb, nb)
        value = recv_cls[0, c, k] * boxes + recv_tgt[0, c, k]
        value = jnp.where(recv_live[0, c, k] != 0, value, -1)
        return jnp.where(lane == boxes + d * cap + c, value, code)

    def add_peer(d, code):
        for c in range(cap):
            code = add_slot(d, c, code)
        return code

    slot_code = jnp.full((1, depth), -1, jnp.int32)
    if nb <= 16:
        for d in range(nb):
            slot_code = add_peer(d, slot_code)
    else:
        slot_code = lax.fori_loop(0, nb, add_peer, slot_code)
    own_code = jnp.transpose(cls_ref[...] * depth + src_ref[...])
    target = lax.broadcasted_iota(jnp.int32, (boxes, depth), 0)
    for q in range(classes):
        total = jnp.where(slot_code == q * boxes + target, 1.0, 0.0)
        for n in range(own_code.shape[1]):
            total += jnp.where(own_code[:, n : n + 1] == q * depth + lane, 1.0, 0.0)
        counts[q * boxes : (q + 1) * boxes, :] = total.astype(BF16)

    over(nb, lambda d: slot_copy(d).wait_recv())
    per_group = group // cap
    for g in range(slots // group):
        rows = arrived[g * per_group : (g + 1) * per_group].reshape(group * rhs, width)
        mixed[:, boxes + g * group : boxes + (g + 1) * group, :] = (
            jnp.dot(swap_slots[...], rows, preferred_element_type=F32)
            .astype(BF16)
            .reshape(rhs, group, width)
        )

    for s in range(rhs):
        held = jnp.dot(counts[...], mixed[s], preferred_element_type=F32).astype(BF16)
        grouped[:, s * boxes : (s + 1) * boxes, :] = held.reshape(classes, boxes, width)

    loads[9].wait()
    total = dot_nt(grouped[0], trans[0])
    for q in range(1, classes):
        total += dot_nt(grouped[q], trans[q])
    high = total.astype(BF16)
    low = (total - high.astype(F32)).astype(BF16)
    near[...] = (
        jnp.dot(swap_back[...], high, preferred_element_type=F32)
        + jnp.dot(swap_back[...], low, preferred_element_type=F32)
    ).reshape(boxes, rhs, width)

    loads[10].wait()
    over(nb, lambda d: top_copy(d).wait_recv())
    far = coupling[box, box] * top
    if nb <= 16:
        for d in range(1, nb):
            far += coupling[box, lax.rem(box - d + nb, nb)] * tops[d].astype(F32)
    else:
        far = lax.fori_loop(
            1,
            nb,
            lambda d, far: far + coupling[box, lax.rem(box - d + nb, nb)] * tops[d].astype(F32),
            far,
        )
    far = far.astype(BF16)
    for m in range(children):
        field = dot_nt(far, down[m])
        for g in range(boxes // children):
            b = g * children + m
            out_ref[b] = (near[b] + field).astype(BF16)

    over(ns, lambda d: part_copy(d).wait_send())
    over(nb, lambda d: slot_copy(d).wait_send())
    over(nb, lambda d: top_copy(d).wait_send())


def local(nb, ns, *args):
    leaves, local_src, local_cls, send_box, recv_tgt, recv_cls, recv_live = args[:7]
    translation, up_maps, down_maps, coupling = args[7:]
    boxes, rhs, width = leaves.shape
    cap = send_box.shape[2]
    classes = translation.shape[0]
    depth = boxes + nb * cap
    rows = boxes * rhs
    vmem = pl.BlockSpec(memory_space=pltpu.VMEM)
    hbm = pl.BlockSpec(memory_space=pltpu.HBM)
    dma = pltpu.SemaphoreType.DMA
    int_vmem = pltpu.VMEM(local_src.shape[::-1], jnp.int32)
    int_smem = pltpu.SMEM((1, cap, nb), jnp.int32)
    operands = (
        leaves,
        local_src.T,
        local_cls.T,
        *(jnp.transpose(a, (0, 2, 1)) for a in (send_box, recv_tgt, recv_cls, recv_live)),
        translation,
        up_maps,
        down_maps,
        coupling,
    )
    return pl.pallas_call(
        functools.partial(kernel, nb, ns),
        out_shape=jax.ShapeDtypeStruct(leaves.shape, BF16),
        in_specs=[hbm] * 11,
        out_specs=vmem,
        scratch_shapes=[
            int_vmem,
            int_vmem,
            int_smem,
            int_smem,
            int_smem,
            int_smem,
            pltpu.SMEM(coupling.shape, F32),
            pltpu.VMEM((boxes, rhs, width), BF16),
            pltpu.VMEM(translation.shape, BF16),
            pltpu.VMEM(up_maps.shape[1:], BF16),
            pltpu.VMEM(down_maps.shape[1:], BF16),
            pltpu.VMEM((nb, cap, rhs, width), BF16),
            pltpu.VMEM((nb, cap, rhs, width), BF16),
            pltpu.VMEM((rhs, width), BF16),
            pltpu.VMEM((ns, rhs, width), BF16),
            pltpu.VMEM((rhs, width), BF16),
            pltpu.VMEM((nb, rhs, width), BF16),
            pltpu.VMEM((rhs, depth, width), BF16),
            pltpu.VMEM((classes * boxes, depth), BF16),
            pltpu.VMEM((classes, rhs * boxes, width), BF16),
            pltpu.VMEM((boxes, rhs, width), F32),
            pltpu.VMEM((rows, rows), BF16),
            pltpu.VMEM((16 * rhs, 16 * rhs), BF16),
            pltpu.VMEM((rows, rows), BF16),
            dma((11,)),
            dma((nb,)),
            dma((nb,)),
            dma((ns,)),
            dma((ns,)),
            dma((nb,)),
            dma((nb,)),
        ],
        compiler_params=pltpu.CompilerParams(
            collective_id=0, has_side_effects=True, vmem_limit_bytes=48 * 1024 * 1024
        ),
    )(*(pltpu.with_memory_space_constraint(a, pltpu.HBM) for a in operands))


def solution(mesh):
    dev = ("box", "sub")
    in_specs = (
        P(dev, None, None),
        P(dev, None),
        P(dev, None),
        P(dev, None, None),
        P(dev, None, None),
        P(dev, None, None),
        P(dev, None, None),
        P(),
        P("sub", None, None, None),
        P("sub", None, None, None),
        P(),
    )
    return jax.shard_map(
        functools.partial(local, mesh.shape["box"], mesh.shape["sub"]),
        mesh=mesh,
        in_specs=in_specs,
        out_specs=P(dev, None, None),
        check_vma=False,
    )
```

```python
import functools

import jax
import jax.numpy as jnp
from jax import lax
from jax.experimental import pallas as pl
from jax.experimental.pallas import tpu as pltpu
from jax.sharding import PartitionSpec as P

MESH = pl.DeviceIdType.MESH
F32 = jnp.float32
BF16 = jnp.bfloat16


def dot_nt(a, b):
    return lax.dot_general(a, b, (((1,), (1,)), ((), ())), preferred_element_type=F32)


def swap_matrix(outer, inner):
    size = outer * inner
    row = lax.broadcasted_iota(jnp.int32, (size, 1), 0)
    source = (row % inner) * outer + row // inner
    column = lax.broadcasted_iota(jnp.int32, (size, size), 1)
    return jnp.where(column == source, 1.0, 0.0).astype(BF16)


def kernel(
    nb,
    ns,
    leaves_hbm,
    src_hbm,
    cls_hbm,
    send_hbm,
    tgt_hbm,
    rcls_hbm,
    live_hbm,
    trans_hbm,
    up_hbm,
    down_hbm,
    coupling_hbm,
    out_ref,
    src_ref,
    cls_ref,
    send_box,
    recv_tgt,
    recv_cls,
    recv_live,
    coupling,
    leaves,
    trans,
    up,
    down,
    outgoing,
    arrived,
    part_out,
    parts,
    top_out,
    tops,
    mixed,
    counts,
    grouped,
    near,
    swap_in,
    row_cls,
    spread,
    swap_back,
    load_sem,
    slot_send,
    slot_recv,
    part_send,
    part_recv,
    top_send,
    top_recv,
):
    box = lax.axis_index("box")
    sub = lax.axis_index("sub")
    boxes, rhs, width = leaves.shape
    cap = outgoing.shape[1]
    classes = trans.shape[0]
    children = up.shape[0]
    slots = nb * cap
    group = 16
    rows = group * rhs

    def box_peer(d):
        return (lax.rem(box + d, nb), sub)

    def sub_peer(d):
        return (box, lax.rem(sub + d, ns))

    def over(count, body):
        if count <= 16:
            for d in range(1, count):
                body(d)
        else:
            pl.loop(1, count)(body)

    barrier = pltpu.get_barrier_semaphore()
    over(ns, lambda d: pl.semaphore_signal(barrier, inc=1, device_id=sub_peer(d), device_id_type=MESH))
    over(nb, lambda d: pl.semaphore_signal(barrier, inc=1, device_id=box_peer(d), device_id_type=MESH))

    pairs = (
        (leaves_hbm, leaves),
        (send_hbm, send_box),
        (up_hbm.at[0], up),
        (src_hbm, src_ref),
        (cls_hbm, cls_ref),
        (tgt_hbm, recv_tgt),
        (rcls_hbm, recv_cls),
        (live_hbm, recv_live),
        (coupling_hbm, coupling),
        (trans_hbm, trans),
        (down_hbm.at[0], down),
    )
    loads = [pltpu.make_async_copy(a, b, load_sem.at[n]) for n, (a, b) in enumerate(pairs)]
    for load in loads[:9]:
        load.start()

    swap_in[...] = swap_matrix(rhs, boxes)
    swap_back[...] = swap_matrix(boxes, rhs)

    loads[0].wait()
    for load in loads[9:]:
        load.start()
    loads[1].wait()
    if nb <= 16:
        for d in range(nb):
            for c in range(cap):
                outgoing[d, c] = leaves[send_box[0, c, lax.rem(box + d, nb)]]
    else:

        @pl.loop(0, nb)
        def _(d):
            for c in range(cap):
                outgoing[d, c] = leaves[send_box[0, c, lax.rem(box + d, nb)]]

    for c in range(cap):
        arrived[0, c] = outgoing[0, c]

    pl.semaphore_wait(barrier, nb + ns - 2)

    def part_copy(d):
        return pltpu.make_async_remote_copy(
            src_ref=part_out,
            dst_ref=parts.at[d],
            send_sem=part_send.at[d],
            recv_sem=part_recv.at[d],
            device_id=sub_peer(d),
            device_id_type=MESH,
        )

    def slot_copy(d):
        return pltpu.make_async_remote_copy(
            src_ref=outgoing.at[d],
            dst_ref=arrived.at[d],
            send_sem=slot_send.at[d],
            recv_sem=slot_recv.at[d],
            device_id=box_peer(d),
            device_id_type=MESH,
        )

    def top_copy(d):
        return pltpu.make_async_remote_copy(
            src_ref=top_out,
            dst_ref=tops.at[d],
            send_sem=top_send.at[d],
            recv_sem=top_recv.at[d],
            device_id=box_peer(d),
            device_id_type=MESH,
        )

    over(nb, lambda d: slot_copy(d).start())

    child = leaves[0:children].astype(F32)
    for g in range(1, boxes // children):
        child += leaves[g * children : (g + 1) * children].astype(F32)
    child = child.astype(BF16)

    loads[2].wait()
    part = dot_nt(child[0], up[0])
    for m in range(1, children):
        part += dot_nt(child[m], up[m])
    part_out[...] = part.astype(BF16)
    over(ns, lambda d: part_copy(d).start())

    for load in loads[3:9]:
        load.wait()

    lane = lax.broadcasted_iota(jnp.int32, (1, boxes), 1)
    own_code = jnp.transpose(cls_ref[...] * boxes + src_ref[...])
    for q in range(classes):
        total = jnp.zeros((boxes, boxes), F32)
        for n in range(own_code.shape[1]):
            total += jnp.where(own_code[:, n : n + 1] == q * boxes + lane, 1.0, 0.0)
        counts[q * boxes : (q + 1) * boxes, :] = total.astype(BF16)

    mixed[...] = (
        jnp.dot(
            swap_in[...],
            leaves[...].reshape(boxes * rhs, width),
            preferred_element_type=F32,
        )
        .astype(BF16)
        .reshape(rhs, boxes, width)
    )
    for s in range(rhs):
        held = jnp.dot(counts[...], mixed[s], preferred_element_type=F32).astype(BF16)
        grouped[:, s * boxes : (s + 1) * boxes, :] = held.reshape(classes, boxes, width)

    top = part
    over(ns, lambda d: part_copy(d).wait_recv())
    for d in range(1, ns):
        top += parts[d].astype(F32)
    top_out[...] = top.astype(BF16)
    over(nb, lambda d: top_copy(d).start())


    across = lax.broadcasted_iota(jnp.int32, (1, slots * rhs), 1)

    def place(d, goal):
        k = lax.rem(box - d + nb, nb)
        for c in range(cap):
            first = (d * cap + c) * rhs
            row_cls[pl.ds(first, rhs), :] = jnp.full((rhs, width), recv_cls[0, c, k], jnp.int32)
            aim = jnp.where(recv_live[0, c, k] != 0, recv_tgt[0, c, k] * rhs, -slots * rhs) - first
            inside = (across >= first) & (across < first + rhs)
            goal = jnp.where(inside, across + aim, goal)
        return goal

    goal = jnp.full((1, slots * rhs), -1, jnp.int32)
    if nb <= 16:
        for d in range(nb):
            goal = place(d, goal)
    else:
        goal = lax.fori_loop(0, nb, place, goal)
    target = lax.broadcasted_iota(jnp.int32, (boxes * rhs, slots * rhs), 0)
    spread[...] = jnp.where(target == goal, 1.0, 0.0).astype(BF16)

    loads[9].wait()
    total = dot_nt(grouped[0], trans[0])
    for q in range(1, classes):
        total += dot_nt(grouped[q], trans[q])
    high = total.astype(BF16)
    low = (total - high.astype(F32)).astype(BF16)
    near[...] = (
        jnp.dot(swap_back[...], high, preferred_element_type=F32)
        + jnp.dot(swap_back[...], low, preferred_element_type=F32)
    ).reshape(boxes, rhs, width)

    over(nb, lambda d: slot_copy(d).wait_recv())
    for g in range(slots // group):
        some = arrived[g * group // cap : (g + 1) * group // cap].reshape(rows, width)
        which = row_cls[g * rows : (g + 1) * rows, :]
        moved = dot_nt(some, trans[0])
        for q in range(1, classes):
            moved = jnp.where(which == q, dot_nt(some, trans[q]), moved)
        near[...] += jnp.dot(
            spread[:, g * rows : (g + 1) * rows], moved.astype(BF16), preferred_element_type=F32
        ).reshape(boxes, rhs, width)

    loads[10].wait()
    over(nb, lambda d: top_copy(d).wait_recv())
    far = coupling[box, box] * top
    if nb <= 16:
        for d in range(1, nb):
            far += coupling[box, lax.rem(box - d + nb, nb)] * tops[d].astype(F32)
    else:
        far = lax.fori_loop(
            1,
            nb,
            lambda d, far: far + coupling[box, lax.rem(box - d + nb, nb)] * tops[d].astype(F32),
            far,
        )
    far = far.astype(BF16)
    for m in range(children):
        field = dot_nt(far, down[m])
        for g in range(boxes // children):
            b = g * children + m
            out_ref[b] = (near[b] + field).astype(BF16)

    over(ns, lambda d: part_copy(d).wait_send())
    over(nb, lambda d: slot_copy(d).wait_send())
    over(nb, lambda d: top_copy(d).wait_send())


def local(nb, ns, *args):
    leaves, local_src, local_cls, send_box, recv_tgt, recv_cls, recv_live = args[:7]
    translation, up_maps, down_maps, coupling = args[7:]
    boxes, rhs, width = leaves.shape
    cap = send_box.shape[2]
    classes = translation.shape[0]
    rows = boxes * rhs
    vmem = pl.BlockSpec(memory_space=pltpu.VMEM)
    hbm = pl.BlockSpec(memory_space=pltpu.HBM)
    dma = pltpu.SemaphoreType.DMA
    int_vmem = pltpu.VMEM(local_src.shape[::-1], jnp.int32)
    int_smem = pltpu.SMEM((1, cap, nb), jnp.int32)
    operands = (
        leaves,
        local_src.T,
        local_cls.T,
        *(jnp.transpose(a, (0, 2, 1)) for a in (send_box, recv_tgt, recv_cls, recv_live)),
        translation,
        up_maps,
        down_maps,
        coupling,
    )
    return pl.pallas_call(
        functools.partial(kernel, nb, ns),
        out_shape=jax.ShapeDtypeStruct(leaves.shape, BF16),
        in_specs=[hbm] * 11,
        out_specs=vmem,
        scratch_shapes=[
            int_vmem,
            int_vmem,
            int_smem,
            int_smem,
            int_smem,
            int_smem,
            pltpu.SMEM(coupling.shape, F32),
            pltpu.VMEM((boxes, rhs, width), BF16),
            pltpu.VMEM(translation.shape, BF16),
            pltpu.VMEM(up_maps.shape[1:], BF16),
            pltpu.VMEM(down_maps.shape[1:], BF16),
            pltpu.VMEM((nb, cap, rhs, width), BF16),
            pltpu.VMEM((nb, cap, rhs, width), BF16),
            pltpu.VMEM((rhs, width), BF16),
            pltpu.VMEM((ns, rhs, width), BF16),
            pltpu.VMEM((rhs, width), BF16),
            pltpu.VMEM((nb, rhs, width), BF16),
            pltpu.VMEM((rhs, boxes, width), BF16),
            pltpu.VMEM((classes * boxes, boxes), BF16),
            pltpu.VMEM((classes, rhs * boxes, width), BF16),
            pltpu.VMEM((boxes, rhs, width), F32),
            pltpu.VMEM((rows, rows), BF16),
            pltpu.VMEM((nb * cap * rhs, width), jnp.int32),
            pltpu.VMEM((rows, nb * cap * rhs), BF16),
            pltpu.VMEM((rows, rows), BF16),
            dma((11,)),
            dma((nb,)),
            dma((nb,)),
            dma((ns,)),
            dma((ns,)),
            dma((nb,)),
            dma((nb,)),
        ],
        compiler_params=pltpu.CompilerParams(
            collective_id=0, has_side_effects=True, vmem_limit_bytes=48 * 1024 * 1024
        ),
    )(*(pltpu.with_memory_space_constraint(a, pltpu.HBM) for a in operands))


def solution(mesh):
    dev = ("box", "sub")
    in_specs = (
        P(dev, None, None),
        P(dev, None),
        P(dev, None),
        P(dev, None, None),
        P(dev, None, None),
        P(dev, None, None),
        P(dev, None, None),
        P(),
        P("sub", None, None, None),
        P("sub", None, None, None),
        P(),
    )
    return jax.shard_map(
        functools.partial(local, mesh.shape["box"], mesh.shape["sub"]),
        mesh=mesh,
        in_specs=in_specs,
        out_specs=P(dev, None, None),
        check_vma=False,
    )
```
